32 devices in a mesh: kv: 4 (over y, x), ctx: 8 (over z, core).
Axes of the slice: x: 2, y: 2, z: 4, core: 2. Of those that a mesh axis runs over, the one named last changes fastest.
Arguments:
- queries: bfloat16 [1024, 8192], P('ctx', 'kv'), may hold values from -8 to 8
- key_cache: bfloat16 [32768, 1024], P('ctx', 'kv'), may hold values from -8 to 8
- value_cache: bfloat16 [32768, 1024], P('ctx', 'kv'), may hold values from -6 to 6
- blocks: int32 [8, 8, 32], replicated, may hold values from 0 to 255, as said below
- out_weight: bfloat16 [8192, 8192], P('kv', 'ctx'), may hold values from -0.0625 to 0.0625
Outputs:
- attended: bfloat16 [1024, 8192], P('kv', 'ctx')
The draws below stay inside these ranges and needn't reach their ends.
Inputs may be any that keep to these rules, and one draw needn't show every extreme that they name: blocks[b, h, :] lists 32 distinct key blocks in ascending order, none after block 248 + b and always that block itself; each list names at most 7 of one cache device's 32 blocks, and a quarter of the 8 cache devices get 1, 3, 5 and 7 of its blocks each.
All inputs are finite; a program needn't handle non-finite values.
Results may differ from the reference program's by a relative error of at most 0.012.
Values may be sent and summed in bfloat16 or wider, within the bound.
A program may use at most 64 MiB of HBM per device.

```python
import math
import jax
import jax.numpy as jnp
from jax import lax

D = 8192
HQ = 64
KVH = 8
HD = 128
BLK = 128
QBLK = 8
MOST = 7
BPS = 32
CTX_DEV = 4096
CTX = 32768
NKB = 256
SEL = 32
QTOK = 1024
N_CTX = 8


def draw_queries(key, part):
    shape = (QTOK, HQ * HD)
    values = jax.random.truncated_normal(jax.random.fold_in(key, 1), -6.0, 6.0, shape, jnp.float32)
    return values.astype(jnp.bfloat16)


def draw_key_cache(key, part):
    shape = (CTX, KVH * HD)
    values = jax.random.truncated_normal(jax.random.fold_in(key, 2), -6.0, 6.0, shape, jnp.float32)
    return values.astype(jnp.bfloat16)


def draw_blocks(key, part):
    shards = N_CTX
    base = jax.random.fold_in(key, 21)
    jitter = jax.random.randint(jax.random.fold_in(base, 1), (QBLK, KVH, shards), 0, shards // 2 + 1)
    order = jnp.arange(shards, dtype=jnp.int32)
    ranking = (order + jitter) * shards + order
    rank = jnp.argsort(jnp.argsort(ranking, axis=-1), axis=-1)
    counts = 1 + 2 * (4 * rank // shards)
    local = jnp.arange(BPS, dtype=jnp.int32)
    globals_here = order[:, None] * BPS + local[None, :]
    limit = NKB - QBLK + jnp.arange(QBLK, dtype=jnp.int32)[:, None, None, None]
    candidate = jax.random.randint(jax.random.fold_in(base, 2), (QBLK, KVH, shards, BPS), 0, 1 << 20) * BPS + local
    candidate = jnp.where(globals_here[None, None] == limit, 1 << 30, candidate)
    candidate = jnp.where(globals_here[None, None] > limit, -1, candidate)
    unused, top_index = lax.top_k(candidate, MOST)
    picked = order[:, None] * BPS + top_index
    keep = jnp.arange(MOST, dtype=jnp.int32) < counts[..., None]
    picked = jnp.where(keep, picked, NKB)
    flat = jnp.sort(picked.reshape(QBLK, KVH, shards * MOST), axis=-1)
    return flat[..., :SEL].astype(jnp.int32)


def steps_of(key, shape, cuts, smallest, high):
    level, own = 1.0, jax.random.fold_in(key, 6)
    for axis_at, shards_of in cuts:
        heights = jnp.exp(jax.random.uniform(jax.random.fold_in(own, axis_at), (shards_of,), jnp.float32, smallest / len(cuts), high / len(cuts)))
        level = level * jnp.repeat(heights, shape[axis_at] // shards_of).reshape([-1 if axis == axis_at else 1 for axis in range(len(shape))])
    return level


def normal_values(own_key, dims, deviation, reach, cuts=(), kind=jnp.bfloat16):
    factor_of = steps_of(own_key, dims, cuts, -0.22, 0.18) if cuts else 1.0
    array = jax.random.normal(own_key, dims, jnp.float32) * deviation * factor_of
    return jnp.minimum(jnp.maximum(array, -reach), reach).astype(kind)


def setup_inputs(seed: int = 0) -> dict:
    keys = jax.random.split(jax.random.key(seed), 6)
    queries = draw_queries(jax.random.fold_in(keys[5], 71), 0)
    key_cache = draw_key_cache(jax.random.fold_in(keys[5], 71), 0)
    value_cache = normal_values(keys[2], (CTX, KVH * HD), 1.0, 6.0, ((0, 8), (1, 4)))
    blocks = draw_blocks(jax.random.fold_in(keys[5], 71), 0)
    out_weight = normal_values(keys[4], (HQ * HD, D), (HQ * HD) ** -0.5, 0.0625, ((0, 4), (1, 8)))
    return dict(queries=queries, key_cache=key_cache, value_cache=value_cache, blocks=blocks, out_weight=out_weight)


def shard_partials(queries_all, key_shard, value_shard, block_lists, shard_first, total_keys, head_count):
    query_tokens = queries_all.shape[0]
    blocks_here = key_shard.shape[0] // BLK
    group_size = queries_all.shape[1] // (head_count * HD)
    score_scale = 1.0 / math.sqrt(HD)
    below = lax.optimization_barrier(jnp.sum((block_lists < shard_first).astype(jnp.int32), axis=-1))
    inside = lax.optimization_barrier(jnp.sum(((block_lists >= shard_first) & (block_lists < shard_first + blocks_here)).astype(jnp.int32), axis=-1))
    slot_ids = jnp.arange(MOST, dtype=jnp.int32)
    places = jnp.clip(below[..., None] + slot_ids, 0, block_lists.shape[-1] - 1).astype(jnp.int32)
    picked = jnp.take_along_axis(block_lists, places, axis=-1) - shard_first
    usable = slot_ids < inside[..., None]
    picked = jnp.where(usable, picked, 0).astype(jnp.int32)
    key_blocks = key_shard.reshape(blocks_here, BLK, head_count, HD)
    value_blocks = value_shard.reshape(blocks_here, BLK, head_count, HD)
    offsets = jnp.arange(BLK, dtype=jnp.int32)

    def one_block(inputs):
        block_index, picked_now, usable_now = inputs
        rows_here = lax.dynamic_slice_in_dim(queries_all, block_index * BLK, BLK, 0)
        rows_here = rows_here.reshape(BLK, head_count, group_size, HD).astype(jnp.float32)
        query_pos = total_keys - query_tokens + block_index * BLK + offsets
        head_outputs, head_peaks, head_totals = ([], [], [])
        for head_index in range(head_count):
            chosen = picked_now[head_index]
            keys_taken = key_blocks[chosen, :, head_index, :].reshape(MOST * BLK, HD).astype(jnp.float32)
            values_taken = value_blocks[chosen, :, head_index, :].reshape(MOST * BLK, HD).astype(jnp.float32)
            key_pos = ((shard_first + chosen)[:, None] * BLK + offsets[None, :]).reshape(MOST * BLK)
            live_keys = jnp.repeat(usable_now[head_index], BLK)
            allowed = live_keys[None, :] & (key_pos[None, :] <= query_pos[:, None])
            scores = jnp.einsum('rgd,kd->rgk', rows_here[:, head_index], keys_taken) * score_scale
            scores = jnp.where(allowed[:, None, :], scores, -jnp.inf)
            peak_row = lax.optimization_barrier(jnp.max(scores, axis=-1)).astype(jnp.bfloat16)
            weights = jnp.exp(scores - peak_row.astype(jnp.float32)[..., None])
            total_row = lax.optimization_barrier(jnp.sum(weights, axis=-1)).astype(jnp.bfloat16)
            rounded = weights.astype(jnp.bfloat16).astype(jnp.float32)
            mixed = jnp.einsum('rgk,kd->rgd', rounded, values_taken)
            head_outputs.append((mixed / total_row.astype(jnp.float32)[..., None]).astype(jnp.bfloat16))
            head_peaks.append(peak_row)
            head_totals.append(total_row)
        return (jnp.stack(head_outputs, 1), jnp.stack(head_peaks, 1), jnp.stack(head_totals, 1))
    block_ids = jnp.arange(picked.shape[0], dtype=jnp.int32)
    outputs, peaks, totals = lax.map(one_block, (block_ids, picked, usable))
    heads_all = head_count * group_size
    return (outputs.reshape(query_tokens, heads_all, HD), peaks.reshape(query_tokens, heads_all), totals.reshape(query_tokens, heads_all))

def combine_pair(first, second):
    peak_first, total_first, acc_first = first
    peak_second, total_second, acc_second = second
    peak_joint = jnp.maximum(peak_first, peak_second)
    factor_first = jnp.exp(peak_first - peak_joint)
    factor_second = jnp.exp(peak_second - peak_joint)
    total_joint = total_first * factor_first + total_second * factor_second
    acc_joint = acc_first * factor_first[..., None] + acc_second * factor_second[..., None]
    return (peak_joint, total_joint, acc_joint)

def reference(queries, key_cache, value_cache, blocks, out_weight):

    def advance(carry, shard_index):
        key_shard = lax.dynamic_slice_in_dim(key_cache, shard_index * CTX_DEV, CTX_DEV, 0)
        value_shard = lax.dynamic_slice_in_dim(value_cache, shard_index * CTX_DEV, CTX_DEV, 0)
        outputs, peaks, totals = shard_partials(queries, key_shard, value_shard, blocks, shard_index * BPS, CTX, KVH)
        totals_wide = totals.astype(jnp.float32)
        states_now = (peaks.astype(jnp.float32), totals_wide, outputs.astype(jnp.float32) * totals_wide[..., None])
        return (combine_pair(carry, states_now), None)
    start_state = (jnp.full((QTOK, HQ), -jnp.inf, jnp.float32), jnp.zeros((QTOK, HQ), jnp.float32), jnp.zeros((QTOK, HQ, HD), jnp.float32))
    final_state, unused = lax.scan(advance, start_state, jnp.arange(N_CTX, dtype=jnp.int32))
    attended_heads = (final_state[2] / final_state[1][..., None]).astype(jnp.bfloat16).reshape(QTOK, HQ * HD)
    return jnp.dot(attended_heads, out_weight, preferred_element_type=jnp.float32).astype(jnp.bfloat16)
```

```python
import functools
import math

import jax
import jax.numpy as jnp
from jax import lax
from jax.experimental import pallas as pl
from jax.experimental.pallas import tpu as pltpu
from jax.sharding import PartitionSpec as P

HD = 128
BLK = 128
MOST = 7
COUNTS = (1, 3, 5, 7)
LOG2E = math.log2(math.e)


def attend_kernel(diag_first, heads, picked, counts, last, q_ref, k_ref, v_ref, o_ref, lse_ref):
    head_index, block_index = pl.program_id(0), pl.program_id(1)
    count = counts[block_index, head_index]
    on_diagonal = last[block_index, head_index] == diag_first + block_index
    rows = lax.broadcasted_iota(jnp.int32, (2 * BLK, BLK), 0) % BLK
    columns = lax.broadcasted_iota(jnp.int32, (2 * BLK, BLK), 1)
    lanes = lax.broadcasted_iota(jnp.int32, (BLK, BLK), 1)
    hidden = (columns > rows) & on_diagonal
    scale = LOG2E / math.sqrt(HD)

    def with_count(many):
        places = [
            pl.ds(pl.multiple_of(picked[block_index, head_index, slot] * BLK, BLK), BLK)
            for slot in range(many)
        ]
        keys = jnp.concatenate([k_ref[place, :] for place in places], 0)
        values = jnp.concatenate([v_ref[place, :] for place in places], 0)
        stats = jnp.zeros((BLK, BLK), jnp.float32)
        for pair in range(heads // 2):
            at = [slice((2 * pair + i) * HD, (2 * pair + i + 1) * HD) for i in range(2)]
            rows_now = jnp.concatenate([q_ref[:, a] for a in at], 0)
            scores = lax.dot_general(
                rows_now, keys, (((1,), (1,)), ((), ())), preferred_element_type=jnp.float32
            )
            tail = jnp.where(hidden, -jnp.inf, scores[:, (many - 1) * BLK :])
            scores = jnp.concatenate([scores[:, : (many - 1) * BLK], tail], 1) if many > 1 else tail
            peak = jnp.max(scores, axis=1, keepdims=True) * scale
            weights = jnp.exp2(scores * scale - peak)
            total = jnp.sum(weights, axis=1, keepdims=True)
            mixed = jnp.dot(
                weights.astype(jnp.bfloat16), values, preferred_element_type=jnp.float32
            )
            mixed = (mixed / total).astype(jnp.bfloat16)
            lse = peak + jnp.log2(total)
            for i in range(2):
                part = slice(i * BLK, (i + 1) * BLK)
                o_ref[:, at[i]] = mixed[part]
                stats = jnp.where(lanes == 2 * pair + i, lse[part], stats)
        lse_ref[0] = stats.T[:heads]

    for many in COUNTS:
        pl.when(count == many)(functools.partial(with_count, many))


def attend(queries_all, keys, values, picked, counts, last, diag_first):
    tokens, columns = queries_all.shape
    head_count = keys.shape[1] // HD
    group = columns // (head_count * HD)
    query_blocks = tokens // BLK
    spec = pltpu.PrefetchScalarGridSpec(
        num_scalar_prefetch=3,
        grid=(head_count, query_blocks),
        in_specs=[
            pl.BlockSpec((BLK, group * HD), lambda h, b, *_: (b, h)),
            pl.BlockSpec((keys.shape[0], HD), lambda h, b, *_: (0, h)),
            pl.BlockSpec((keys.shape[0], HD), lambda h, b, *_: (0, h)),
        ],
        out_specs=[
            pl.BlockSpec((BLK, group * HD), lambda h, b, *_: (b, h)),
            pl.BlockSpec((1, group, BLK), lambda h, b, *_: (b, h, 0)),
        ],
    )
    return pl.pallas_call(
        functools.partial(attend_kernel, diag_first, group),
        grid_spec=spec,
        out_shape=[
            jax.ShapeDtypeStruct((tokens, columns), jnp.bfloat16),
            jax.ShapeDtypeStruct((query_blocks, head_count * group, BLK), jnp.float32),
        ],
        compiler_params=pltpu.CompilerParams(vmem_limit_bytes=40 * 2**20),
        name="attend",
    )(picked, counts, last, queries_all, keys, values)


def choose(blocks, head_count, shard_first, blocks_here):
    lists = lax.dynamic_slice_in_dim(blocks, lax.axis_index("kv") * head_count, head_count, 1)
    local = lists - shard_first
    below = jnp.sum((local < 0).astype(jnp.int32), axis=-1)
    counts = jnp.sum(((local >= 0) & (local < blocks_here)).astype(jnp.int32), axis=-1)
    slots = jnp.arange(MOST, dtype=jnp.int32)
    places = jnp.arange(blocks.shape[-1], dtype=jnp.int32)
    here = places == (below[..., None] + slots)[..., None]
    picked = jnp.sum(jnp.where(here, local[:, :, None, :], 0), axis=-1)
    picked = jnp.clip(picked, 0, blocks_here - 1)
    last = jnp.sum(jnp.where(slots == (counts - 1)[..., None], picked, 0), axis=-1)
    return picked, counts, last + shard_first


def on_device(queries, key_cache, value_cache, blocks, out_weight):
    head_count = key_cache.shape[1] // HD
    shards = lax.axis_size("ctx")
    blocks_here = key_cache.shape[0] // BLK
    tokens_each = queries.shape[0]
    tokens = tokens_each * shards
    shard_first = lax.axis_index("ctx") * blocks_here
    picked, counts, last = choose(blocks, head_count, shard_first, blocks_here)
    queries_all = lax.all_gather(queries, "ctx", axis=0, tiled=True)
    diag_first = shards * blocks_here - tokens // BLK
    outputs, lse = attend(
        queries_all, key_cache, value_cache, picked, counts, last, diag_first
    )
    outputs = lax.all_to_all(
        outputs.reshape(shards, tokens_each, -1), "ctx", split_axis=0, concat_axis=0, tiled=True
    )
    heads = lse.shape[1]
    lse = lse.transpose(0, 2, 1).reshape(shards, tokens_each, heads)
    lse = lax.all_to_all(lse, "ctx", split_axis=0, concat_axis=0, tiled=True)
    shares = jnp.exp2(lse - jnp.max(lse, axis=0))
    shares = shares / jnp.sum(shares, axis=0)
    outputs = outputs.reshape(shards, tokens_each, heads, HD).astype(jnp.float32)
    merged = jnp.sum(shares[..., None] * outputs, axis=0).astype(jnp.bfloat16)
    merged = merged.reshape(tokens_each, heads * HD)
    projected = jnp.dot(
        lax.all_gather(merged, "ctx", axis=0, tiled=True),
        out_weight,
        preferred_element_type=jnp.float32,
    )
    return lax.psum_scatter(projected.astype(jnp.bfloat16), "kv", scatter_dimension=0, tiled=True)


def solution(mesh):
    placed = (P("ctx", "kv"), P("ctx", "kv"), P("ctx", "kv"), P(), P("kv", "ctx"))
    return jax.shard_map(
        on_device, mesh=mesh, in_specs=placed, out_specs=P("kv", "ctx"), check_vma=False
    )
```

```python
import math

import jax
import jax.numpy as jnp
from jax import lax
from jax.experimental import pallas as pl
from jax.experimental.pallas import tpu as pltpu
from jax.sharding import PartitionSpec as P

HD = 128
BLK = 128
MOST = 7
LOG2E = math.log2(math.e)
MESH = pl.DeviceIdType.MESH


def layer_kernel(
    shards,
    groups,
    picked,
    biases,
    q_ref,
    k_ref,
    v_ref,
    w_hbm,
    out_ref,
    q_all,
    part,
    part_lse,
    pair_in,
    pair_lse,
    stage,
    stage_lse,
    chip_in,
    chip_lse,
    merged_all,
    weight,
    projected,
    group_in,
    q_send,
    q_recv,
    m_send,
    m_recv,
    pair_send,
    pair_recv,
    pair_lse_send,
    pair_lse_recv,
    chip_send,
    chip_recv,
    chip_lse_send,
    chip_lse_recv,
    group_send,
    group_recv,
    w_sem,
):
    me, group_me = lax.axis_index("ctx"), lax.axis_index("kv")
    chips = shards // 2
    chip, core = me // 2, me % 2
    partner = chip * 2 + 1 - core
    tokens = q_ref.shape[0]
    columns = q_ref.shape[1]
    heads = columns // HD
    lists = k_ref.shape[2] // HD
    per_list = heads // lists
    per_group = shards // groups
    scale = LOG2E / math.sqrt(HD)

    weight_copy = pltpu.make_async_copy(w_hbm, weight, w_sem)
    weight_copy.start()

    barrier = pltpu.get_barrier_semaphore()
    pl.semaphore_signal(barrier, inc=1, device_id={"ctx": partner}, device_id_type=MESH)
    for step in range(1, chips):
        other = lax.rem(chip + step, chips) * 2 + core
        pl.semaphore_signal(barrier, inc=1, device_id={"ctx": other}, device_id_type=MESH)
    for step in range(1, groups):
        other = lax.rem(group_me + step, groups)
        pl.semaphore_signal(barrier, inc=1, device_id={"kv": other}, device_id_type=MESH)
    pl.semaphore_wait(barrier, chips + groups - 1)

    def remote(source, target, send, recv, where):
        return pltpu.make_async_remote_copy(
            src_ref=source,
            dst_ref=target,
            send_sem=send,
            recv_sem=recv,
            device_id=where,
            device_id_type=MESH,
        )

    def along(buffer, send, recv, slot, way):
        target = {0: me + 2, 1: me - 2, 2: partner}[way]
        return remote(
            buffer.at[slot], buffer.at[slot], send.at[way, slot], recv.at[slot], {"ctx": target}
        )

    def spread(buffer, send, recv, step):
        def pass_on(slot, way, allowed):
            @pl.when(allowed)
            def _():
                along(buffer, send, recv, slot, way).start()

        low, high = chip - step, chip + step

        @pl.when(low >= 0)
        def _():
            slot = low * 2 + core

            @pl.when(step > 0)
            def _():
                along(buffer, send, recv, slot, 0).wait_recv()

            pass_on(slot, 0, chip + 1 < chips)
            pass_on(slot, 2, step >= 0)

        @pl.when(high < chips)
        def _():
            slot = high * 2 + core

            @pl.when(step > 0)
            def _():
                along(buffer, send, recv, slot, 1).wait_recv()

            pass_on(slot, 1, chip >= 1)
            pass_on(slot, 2, step > 0)

    def finish_spread(buffer, send, recv):
        def one(at, carry):
            slot = at * 2 + core

            @pl.when((at <= chip) & (chip + 1 < chips))
            def _():
                along(buffer, send, recv, slot, 0).wait_send()

            @pl.when((at >= chip) & (chip >= 1))
            def _():
                along(buffer, send, recv, slot, 1).wait_send()

            along(buffer, send, recv, slot, 2).wait_send()
            return carry

        lax.fori_loop(0, chips, one, 0)

    def pair_copies(at):
        slot = at * 2 + 1 - core
        where = {"ctx": partner}
        return (
            remote(part.at[slot], pair_in.at[at], pair_send.at[at], pair_recv.at[at], where),
            remote(
                part_lse.at[slot],
                pair_lse.at[at],
                pair_lse_send.at[at],
                pair_lse_recv.at[at],
                where,
            ),
        )

    def chip_copies(source, target):
        where = {"ctx": target * 2 + core}
        return (
            remote(
                stage.at[target],
                chip_in.at[source],
                chip_send.at[target],
                chip_recv.at[source],
                where,
            ),
            remote(
                stage_lse.at[target],
                chip_lse.at[source],
                chip_lse_send.at[target],
                chip_lse_recv.at[source],
                where,
            ),
        )

    def group_copy(slot, source):
        inside = slot % per_group
        return remote(
            projected.at[slot],
            group_in.at[source, inside],
            group_send.at[slot],
            group_recv.at[source, inside],
            {"kv": slot // per_group},
        )

    def attend(slot):
        first = slot * tokens
        block_index, offset = first // BLK, first % BLK
        stack = max(1, min(per_list, 2 * BLK // tokens))
        rows = lax.broadcasted_iota(jnp.int32, (stack * tokens, BLK), 0) % tokens + offset
        places = lax.broadcasted_iota(jnp.int32, (stack * tokens, BLK), 1)
        lanes = lax.broadcasted_iota(jnp.int32, (tokens, BLK), 1)
        stats = jnp.zeros((tokens, BLK), jnp.float32)
        for index in range(lists):
            chosen = [picked[block_index, index, at] for at in range(MOST)]
            bias = [biases[block_index, index, at] for at in range(MOST)]
            causal = jnp.where(places > rows, bias[0], 0.0)
            here = slice(index * HD, (index + 1) * HD)
            keys = jnp.concatenate([k_ref[one, :, here] for one in chosen], 0)
            values = jnp.concatenate([v_ref[one, :, here] for one in chosen], 0)
            for begin in range(index * per_list, (index + 1) * per_list, stack):
                at = [slice(g * HD, (g + 1) * HD) for g in range(begin, begin + stack)]
                queries = jnp.concatenate([q_all[slot, :, a] for a in at], 0)
                scores = lax.dot_general(
                    queries, keys, (((1,), (1,)), ((), ())), preferred_element_type=jnp.float32
                )
                pieces = [scores[:, :BLK] + causal]
                for s in range(1, MOST):
                    pieces.append(scores[:, s * BLK : (s + 1) * BLK] + bias[s])
                scores = jnp.concatenate(pieces, 1)
                peak = jnp.max(scores, axis=1, keepdims=True) * scale
                weights = jnp.exp2(scores * scale - peak)
                total = jnp.sum(weights, axis=1, keepdims=True)
                mixed = jnp.dot(
                    weights.astype(jnp.bfloat16), values, preferred_element_type=jnp.float32
                )
                mixed = (mixed / total).astype(jnp.bfloat16)
                lse = peak + jnp.log2(total)
                for i in range(stack):
                    mine = slice(i * tokens, (i + 1) * tokens)
                    part[slot, :, at[i]] = mixed[mine]
                    stats = jnp.where(lanes == begin + i, lse[mine], stats)
        part_lse[slot] = stats.T[:heads]

    def merge_pair(at):
        slot = at * 2 + core
        for copy in pair_copies(at):
            copy.wait_recv()
        own, other = part_lse[slot], pair_lse[at]
        top = jnp.maximum(own, other)
        own, other = jnp.exp2(own - top), jnp.exp2(other - top)
        total = own + other
        joint = top + jnp.log2(total)
        own, other = (own / total).T, (other / total).T

        def store(to, to_lse, place):
            to_lse[place] = joint
            for g in range(heads):
                a = slice(g * HD, (g + 1) * HD)
                both = own[:, g : g + 1] * part[slot, :, a].astype(jnp.float32)
                both += other[:, g : g + 1] * pair_in[at, :, a].astype(jnp.float32)
                to[place, :, a] = both.astype(jnp.bfloat16)

        @pl.when(at == chip)
        def _():
            store(chip_in, chip_lse, chip)

        @pl.when(at != chip)
        def _():
            store(stage, stage_lse, at)
            for copy in chip_copies(chip, at):
                copy.start()

    def each(step, visit):
        def one(index, carry):
            side, own_core = index % 2, index // 2
            at = jnp.where(side == 0, chip - step, chip + step)
            valid = (at >= 0) & (at < chips) & ((step > 0) | (side == 0))

            @pl.when(valid)
            def _():
                visit(at, own_core)

            return carry

        return one

    q_all[me] = q_ref[...]

    def attend_step(step, carry):
        spread(q_all, q_send, q_recv, step)

        def visit(at, own_core):
            slot = at * 2 + jnp.where(own_core == 1, core, 1 - core)

            @pl.when(own_core == 0)
            def _():
                along(q_all, q_send, q_recv, slot, 2).wait_recv()

            attend(slot)

            @pl.when(own_core == 0)
            def _():
                for copy in pair_copies(at):
                    copy.start()

        lax.fori_loop(0, 4, each(step, visit), 0)
        lax.fori_loop(0, 2, each(step, lambda at, own_core: merge_pair(at)), 0)
        return carry

    lax.fori_loop(0, chips, attend_step, 0)

    def receive(step, carry):
        source = lax.rem(chip + step, chips)
        for copy in chip_copies(source, chip):
            copy.wait_recv()
        return carry

    lax.fori_loop(1, chips, receive, 0)
    top = chip_lse[0]
    for c in range(1, chips):
        top = jnp.maximum(top, chip_lse[c])
    shares = [jnp.exp2(chip_lse[c] - top) for c in range(chips)]
    total = shares[0]
    for c in range(1, chips):
        total = total + shares[c]
    shares = [(share / total).T for share in shares]
    for g in range(heads):
        a = slice(g * HD, (g + 1) * HD)
        summed = shares[0][:, g : g + 1] * chip_in[0, :, a].astype(jnp.float32)
        for c in range(1, chips):
            summed += shares[c][:, g : g + 1] * chip_in[c, :, a].astype(jnp.float32)
        merged_all[me, :, a] = summed.astype(jnp.bfloat16)

    weight_copy.wait()

    def project_step(step, carry):
        spread(merged_all, m_send, m_recv, step)

        def visit(at, own_core):
            slot = at * 2 + jnp.where(own_core == 1, 1 - core, core)

            @pl.when(own_core == 1)
            def _():
                along(merged_all, m_send, m_recv, slot, 2).wait_recv()

            projected[slot] = jnp.dot(
                merged_all[slot], weight[...], preferred_element_type=jnp.float32
            ).astype(jnp.bfloat16)

            @pl.when(slot // per_group != group_me)
            def _():
                group_copy(slot, group_me).start()

        lax.fori_loop(0, 4, each(step, visit), 0)
        return carry

    lax.fori_loop(0, chips, project_step, 0)

    def gather_groups(inside, carry):
        total = projected[group_me * per_group + inside].astype(jnp.float32)
        for step in range(1, groups):
            source = lax.rem(group_me + step, groups)
            group_copy(group_me * per_group + inside, source).wait_recv()
            total += group_in[source, inside].astype(jnp.float32)
        out_ref[pl.ds(pl.multiple_of(inside * tokens, tokens), tokens), :] = total.astype(
            out_ref.dtype
        )
        return carry

    lax.fori_loop(0, per_group, gather_groups, 0)

    finish_spread(q_all, q_send, q_recv)
    finish_spread(merged_all, m_send, m_recv)

    def finish_chips(at, carry):
        for copy in pair_copies(at):
            copy.wait_send()

        @pl.when(at != chip)
        def _():
            for copy in chip_copies(chip, at):
                copy.wait_send()

        return carry

    lax.fori_loop(0, chips, finish_chips, 0)

    def finish_groups(slot, carry):
        @pl.when(slot // per_group != group_me)
        def _():
            group_copy(slot, group_me).wait_send()

        return carry

    lax.fori_loop(0, shards, finish_groups, 0)


def layer(queries, keys, values, picked, biases, out_weight, shards, groups):
    tokens, columns = queries.shape
    heads = columns // HD
    chips = shards // 2
    wide = out_weight.shape[1]
    per_group = shards // groups
    half, full = jnp.bfloat16, jnp.float32
    dma = pltpu.SemaphoreType.DMA
    smem = pl.BlockSpec(memory_space=pltpu.SMEM)
    vmem = pl.BlockSpec(memory_space=pltpu.VMEM)

    def body(*refs):
        layer_kernel(shards, groups, *refs)

    return pl.pallas_call(
        body,
        in_specs=[smem] * 2 + [vmem] * 3 + [pl.BlockSpec(memory_space=pl.ANY)],
        out_specs=vmem,
        out_shape=jax.ShapeDtypeStruct((per_group * tokens, wide), half),
        scratch_shapes=[
            pltpu.VMEM((shards, tokens, columns), half),
            pltpu.VMEM((shards, tokens, columns), half),
            pltpu.VMEM((shards, heads, tokens), full),
            pltpu.VMEM((chips, tokens, columns), half),
            pltpu.VMEM((chips, heads, tokens), full),
            pltpu.VMEM((chips, tokens, columns), half),
            pltpu.VMEM((chips, heads, tokens), full),
            pltpu.VMEM((chips, tokens, columns), half),
            pltpu.VMEM((chips, heads, tokens), full),
            pltpu.VMEM((shards, tokens, columns), half),
            pltpu.VMEM(out_weight.shape, half),
            pltpu.VMEM((shards, tokens, wide), half),
            pltpu.VMEM((groups, per_group, tokens, wide), half),
            dma((3, shards)),
            dma((shards,)),
            dma((3, shards)),
            dma((shards,)),
            dma((chips,)),
            dma((chips,)),
            dma((chips,)),
            dma((chips,)),
            dma((chips,)),
            dma((chips,)),
            dma((chips,)),
            dma((chips,)),
            dma((shards,)),
            dma((groups, per_group)),
            dma,
        ],
        compiler_params=pltpu.CompilerParams(
            collective_id=0, has_side_effects=True, vmem_limit_bytes=56 * 2**20
        ),
        name="layer",
    )(picked, biases, queries, keys, values, out_weight)


def choose(blocks, head_count, shard_first, blocks_here, diag_first):
    lists = lax.dynamic_slice_in_dim(blocks, lax.axis_index("kv") * head_count, head_count, 1)
    local = lists - shard_first
    below = jnp.sum((local < 0).astype(jnp.int32), axis=-1)
    counts = jnp.sum(((local >= 0) & (local < blocks_here)).astype(jnp.int32), axis=-1)
    slots = jnp.arange(MOST, dtype=jnp.int32)
    places = jnp.arange(blocks.shape[-1], dtype=jnp.int32)
    here = places == ((below + counts - 1)[..., None] - slots)[..., None]
    picked = jnp.sum(jnp.where(here, local[:, :, None, :], 0), axis=-1)
    picked = jnp.clip(picked, 0, blocks_here - 1)
    query_block = jnp.arange(blocks.shape[0], dtype=jnp.int32)[:, None]
    diagonal = picked[..., 0] + shard_first == diag_first + query_block
    barred = jnp.where(slots == 0, diagonal[..., None], slots >= counts[..., None])
    return picked, jnp.where(barred, -jnp.inf, 0.0).astype(jnp.float32)


def on_device(queries, key_cache, value_cache, blocks, out_weight):
    head_count = key_cache.shape[1] // HD
    shards, groups = lax.axis_size("ctx"), lax.axis_size("kv")
    blocks_here = key_cache.shape[0] // BLK
    shard_first = lax.axis_index("ctx") * blocks_here
    diag_first = shards * blocks_here - queries.shape[0] * shards // BLK
    picked, biases = choose(blocks, head_count, shard_first, blocks_here, diag_first)
    keys = key_cache.reshape(blocks_here, BLK, -1)
    values = value_cache.reshape(blocks_here, BLK, -1)
    return layer(queries, keys, values, picked, biases, out_weight, shards, groups)


def solution(mesh):
    placed = (P("ctx", "kv"), P("ctx", "kv"), P("ctx", "kv"), P(), P("kv", "ctx"))
    return jax.shard_map(
        on_device, mesh=mesh, in_specs=placed, out_specs=P("kv", "ctx"), check_vma=False
    )
```

```python
import math

import jax
import jax.numpy as jnp
from jax import lax
from jax.experimental import pallas as pl
from jax.experimental.pallas import tpu as pltpu
from jax.sharding import PartitionSpec as P

HD = 128
BLK = 128
MOST = 7
LOG2E = math.log2(math.e)
MESH = pl.DeviceIdType.MESH


def layer_kernel(
    shards,
    groups,
    picked,
    biases,
    q_ref,
    k_ref,
    v_ref,
    w_hbm,
    out_ref,
    q_all,
    part,
    part_lse,
    pair_in,
    pair_lse,
    stage,
    stage_lse,
    chip_in,
    chip_lse,
    merged_all,
    weight,
    projected,
    group_in,
    q_send,
    q_recv,
    m_send,
    m_recv,
    pair_send,
    pair_recv,
    pair_lse_send,
    pair_lse_recv,
    chip_send,
    chip_recv,
    chip_lse_send,
    chip_lse_recv,
    group_send,
    group_recv,
    w_sem,
):
    me, group_me = lax.axis_index("ctx"), lax.axis_index("kv")
    chips = shards // 2
    chip, core = me // 2, me % 2
    partner = chip * 2 + 1 - core
    tokens = q_ref.shape[0]
    columns = q_ref.shape[1]
    heads = columns // HD
    lists = k_ref.shape[2] // HD
    per_list = heads // lists
    per_group = shards // groups
    scale = LOG2E / math.sqrt(HD)

    weight_copy = pltpu.make_async_copy(w_hbm, weight, w_sem)
    weight_copy.start()

    barrier = pltpu.get_barrier_semaphore()
    pl.semaphore_signal(barrier, inc=1, device_id={"ctx": partner}, device_id_type=MESH)
    for step in range(1, chips):
        other = lax.rem(chip + step, chips) * 2 + core
        pl.semaphore_signal(barrier, inc=1, device_id={"ctx": other}, device_id_type=MESH)
    for step in range(1, groups):
        other = lax.rem(group_me + step, groups)
        pl.semaphore_signal(barrier, inc=1, device_id={"kv": other}, device_id_type=MESH)
    pl.semaphore_wait(barrier, chips + groups - 1)

    def remote(source, target, send, recv, where):
        return pltpu.make_async_remote_copy(
            src_ref=source,
            dst_ref=target,
            send_sem=send,
            recv_sem=recv,
            device_id=where,
            device_id_type=MESH,
        )

    def along(buffer, send, recv, slot, way):
        target = {0: me + 2, 1: me - 2, 2: partner}[way]
        return remote(
            buffer.at[slot], buffer.at[slot], send.at[way, slot], recv.at[slot], {"ctx": target}
        )

    def spread(buffer, send, recv, step):
        def pass_on(slot, way, allowed):
            @pl.when(allowed)
            def _():
                along(buffer, send, recv, slot, way).start()

        low, high = chip - step, chip + step

        @pl.when(low >= 0)
        def _():
            slot = low * 2 + core

            @pl.when(step > 0)
            def _():
                along(buffer, send, recv, slot, 0).wait_recv()

            pass_on(slot, 0, chip + 1 < chips)
            pass_on(slot, 2, step >= 0)

        @pl.when(high < chips)
        def _():
            slot = high * 2 + core

            @pl.when(step > 0)
            def _():
                along(buffer, send, recv, slot, 1).wait_recv()

            pass_on(slot, 1, chip >= 1)
            pass_on(slot, 2, step > 0)

    def finish_spread(buffer, send, recv):
        def one(at, carry):
            slot = at * 2 + core

            @pl.when((at <= chip) & (chip + 1 < chips))
            def _():
                along(buffer, send, recv, slot, 0).wait_send()

            @pl.when((at >= chip) & (chip >= 1))
            def _():
                along(buffer, send, recv, slot, 1).wait_send()

            along(buffer, send, recv, slot, 2).wait_send()
            return carry

        lax.fori_loop(0, chips, one, 0)

    def pair_copies(at):
        slot = at * 2 + 1 - core
        where = {"ctx": partner}
        return (
            remote(part.at[slot], pair_in.at[at], pair_send.at[at], pair_recv.at[at], where),
            remote(
                part_lse.at[slot],
                pair_lse.at[at],
                pair_lse_send.at[at],
                pair_lse_recv.at[at],
                where,
            ),
        )

    def chip_copies(source, target):
        where = {"ctx": target * 2 + core}
        return (
            remote(
                stage.at[target],
                chip_in.at[source],
                chip_send.at[target],
                chip_recv.at[source],
                where,
            ),
            remote(
                stage_lse.at[target],
                chip_lse.at[source],
                chip_lse_send.at[target],
                chip_lse_recv.at[source],
                where,
            ),
        )

    def group_copy(slot, source):
        inside = slot % per_group
        return remote(
            projected.at[slot],
            group_in.at[source, inside],
            group_send.at[slot],
            group_recv.at[source, inside],
            {"kv": slot // per_group},
        )

    def attend(slot):
        first = slot * tokens
        block_index, offset = first // BLK, first % BLK
        stack = max(1, min(per_list, 2 * BLK // tokens))
        rows = lax.broadcasted_iota(jnp.int32, (stack * tokens, BLK), 0) % tokens + offset
        places = lax.broadcasted_iota(jnp.int32, (stack * tokens, BLK), 1)
        lanes = lax.broadcasted_iota(jnp.int32, (tokens, BLK), 1)
        stats = jnp.zeros((tokens, BLK), jnp.float32)
        for index in range(lists):
            chosen = [picked[block_index, index, at] for at in range(MOST)]
            bias = [biases[block_index, index, at] for at in range(MOST)]
            causal = jnp.where(places > rows, bias[0], 0.0)
            here = slice(index * HD, (index + 1) * HD)
            keys = jnp.concatenate([k_ref[one, :, here] for one in chosen], 0)
            values = jnp.concatenate([v_ref[one, :, here] for one in chosen], 0)
            for begin in range(index * per_list, (index + 1) * per_list, stack):
                at = [slice(g * HD, (g + 1) * HD) for g in range(begin, begin + stack)]
                queries = jnp.concatenate([q_all[slot, :, a] for a in at], 0)
                scores = lax.dot_general(
                    queries, keys, (((1,), (1,)), ((), ())), preferred_element_type=jnp.float32
                )
                pieces = [scores[:, :BLK] + causal]
                for s in range(1, MOST):
                    pieces.append(scores[:, s * BLK : (s + 1) * BLK] + bias[s])
                scores = jnp.concatenate(pieces, 1)
                peak = jnp.max(scores, axis=1, keepdims=True) * scale
                weights = jnp.exp2(scores * scale - peak)
                total = jnp.sum(weights, axis=1, keepdims=True)
                mixed = jnp.dot(
                    weights.astype(jnp.bfloat16), values, preferred_element_type=jnp.float32
                )
                mixed = (mixed / total).astype(jnp.bfloat16)
                lse = peak + jnp.log2(total)
                for i in range(stack):
                    mine = slice(i * tokens, (i + 1) * tokens)
                    part[slot, :, at[i]] = mixed[mine]
                    stats = jnp.where(lanes == begin + i, lse[mine], stats)
        part_lse[slot] = stats.T[:heads]

    def merge_pair(at):
        slot = at * 2 + core
        for copy in pair_copies(at):
            copy.wait_recv()
        own, other = part_lse[slot], pair_lse[at]
        top = jnp.maximum(own, other)
        own, other = jnp.exp2(own - top), jnp.exp2(other - top)
        total = own + other
        joint = top + jnp.log2(total)
        own, other = (own / total).T, (other / total).T

        def store(to, to_lse, place):
            to_lse[place] = joint
            for g in range(heads):
                a = slice(g * HD, (g + 1) * HD)
                both = own[:, g : g + 1] * part[slot, :, a].astype(jnp.float32)
                both += other[:, g : g + 1] * pair_in[at, :, a].astype(jnp.float32)
                to[place, :, a] = both.astype(jnp.bfloat16)

        @pl.when(at == chip)
        def _():
            store(chip_in, chip_lse, chip)

        @pl.when(at != chip)
        def _():
            store(stage, stage_lse, at)
            for copy in chip_copies(chip, at):
                copy.start()

    def two_sides(step, visit, between):
        def one(turn, carry):
            side = jnp.where(chip - step >= 0, turn, 1 - turn)
            at = jnp.where(side == 0, chip - step, chip + step)

            @pl.when((at >= 0) & (at < chips) & ((step > 0) | (turn == 0)))
            def _():
                visit(at)

            @pl.when(turn == 0)
            def _():
                between(step + 1)

            return carry

        lax.fori_loop(0, 2, one, 0)

    q_all[me] = q_ref[...]
    spread(q_all, q_send, q_recv, 0)

    def attend_chip(at):
        def one(own_core, carry):
            slot = at * 2 + jnp.where(own_core == 1, core, 1 - core)

            @pl.when(own_core == 0)
            def _():
                along(q_all, q_send, q_recv, slot, 2).wait_recv()

            attend(slot)

            @pl.when(own_core == 0)
            def _():
                for copy in pair_copies(at):
                    copy.start()

            return carry

        lax.fori_loop(0, 2, one, 0)
        merge_pair(at)

    def attend_step(step, carry):
        two_sides(step, attend_chip, lambda later: spread(q_all, q_send, q_recv, later))
        return carry

    lax.fori_loop(0, chips, attend_step, 0)

    def receive(step, carry):
        source = lax.rem(chip + step, chips)
        for copy in chip_copies(source, chip):
            copy.wait_recv()
        return carry

    lax.fori_loop(1, chips, receive, 0)
    top = chip_lse[0]
    for c in range(1, chips):
        top = jnp.maximum(top, chip_lse[c])
    shares = [jnp.exp2(chip_lse[c] - top) for c in range(chips)]
    total = shares[0]
    for c in range(1, chips):
        total = total + shares[c]
    shares = [(share / total).T for share in shares]
    for g in range(heads):
        a = slice(g * HD, (g + 1) * HD)
        summed = shares[0][:, g : g + 1] * chip_in[0, :, a].astype(jnp.float32)
        for c in range(1, chips):
            summed += shares[c][:, g : g + 1] * chip_in[c, :, a].astype(jnp.float32)
        merged_all[me, :, a] = summed.astype(jnp.bfloat16)

    weight_copy.wait()

    spread(merged_all, m_send, m_recv, 0)

    def project_chip(at):
        along(merged_all, m_send, m_recv, at * 2 + 1 - core, 2).wait_recv()
        both = pl.ds(at * 2, 2)
        product = jnp.dot(
            merged_all[both].reshape(2 * tokens, columns),
            weight[...],
            preferred_element_type=jnp.float32,
        )
        projected[both] = product.astype(jnp.bfloat16).reshape(2, tokens, -1)

        @pl.when(at * 2 // per_group != group_me)
        def _():
            for i in range(2):
                group_copy(at * 2 + i, group_me).start()

    def project_step(step, carry):
        two_sides(step, project_chip, lambda later: spread(merged_all, m_send, m_recv, later))
        return carry

    lax.fori_loop(0, chips, project_step, 0)

    def gather_groups(inside, carry):
        total = projected[group_me * per_group + inside].astype(jnp.float32)
        for step in range(1, groups):
            source = lax.rem(group_me + step, groups)
            group_copy(group_me * per_group + inside, source).wait_recv()
            total += group_in[source, inside].astype(jnp.float32)
        out_ref[pl.ds(pl.multiple_of(inside * tokens, tokens), tokens), :] = total.astype(
            out_ref.dtype
        )
        return carry

    lax.fori_loop(0, per_group, gather_groups, 0)

    finish_spread(q_all, q_send, q_recv)
    finish_spread(merged_all, m_send, m_recv)

    def finish_chips(at, carry):
        for copy in pair_copies(at):
            copy.wait_send()

        @pl.when(at != chip)
        def _():
            for copy in chip_copies(chip, at):
                copy.wait_send()

        return carry

    lax.fori_loop(0, chips, finish_chips, 0)

    def finish_groups(slot, carry):
        @pl.when(slot // per_group != group_me)
        def _():
            group_copy(slot, group_me).wait_send()

        return carry

    lax.fori_loop(0, shards, finish_groups, 0)


def layer(queries, keys, values, picked, biases, out_weight, shards, groups):
    tokens, columns = queries.shape
    heads = columns // HD
    chips = shards // 2
    wide = out_weight.shape[1]
    per_group = shards // groups
    half, full = jnp.bfloat16, jnp.float32
    dma = pltpu.SemaphoreType.DMA
    smem = pl.BlockSpec(memory_space=pltpu.SMEM)
    vmem = pl.BlockSpec(memory_space=pltpu.VMEM)

    def body(*refs):
        layer_kernel(shards, groups, *refs)

    return pl.pallas_call(
        body,
        in_specs=[smem] * 2 + [vmem] * 3 + [pl.BlockSpec(memory_space=pl.ANY)],
        out_specs=vmem,
        out_shape=jax.ShapeDtypeStruct((per_group * tokens, wide), half),
        scratch_shapes=[
            pltpu.VMEM((shards, tokens, columns), half),
            pltpu.VMEM((shards, tokens, columns), half),
            pltpu.VMEM((shards, heads, tokens), full),
            pltpu.VMEM((chips, tokens, columns), half),
            pltpu.VMEM((chips, heads, tokens), full),
            pltpu.VMEM((chips, tokens, columns), half),
            pltpu.VMEM((chips, heads, tokens), full),
            pltpu.VMEM((chips, tokens, columns), half),
            pltpu.VMEM((chips, heads, tokens), full),
            pltpu.VMEM((shards, tokens, columns), half),
            pltpu.VMEM(out_weight.shape, half),
            pltpu.VMEM((shards, tokens, wide), half),
            pltpu.VMEM((groups, per_group, tokens, wide), half),
            dma((3, shards)),
            dma((shards,)),
            dma((3, shards)),
            dma((shards,)),
            dma((chips,)),
            dma((chips,)),
            dma((chips,)),
            dma((chips,)),
            dma((chips,)),
            dma((chips,)),
            dma((chips,)),
            dma((chips,)),
            dma((shards,)),
            dma((groups, per_group)),
            dma,
        ],
        compiler_params=pltpu.CompilerParams(
            collective_id=0, has_side_effects=True, vmem_limit_bytes=56 * 2**20
        ),
        name="layer",
    )(picked, biases, queries, keys, values, out_weight)


def choose(blocks, head_count, shard_first, blocks_here, diag_first):
    lists = lax.dynamic_slice_in_dim(blocks, lax.axis_index("kv") * head_count, head_count, 1)
    local = lists - shard_first
    below = jnp.sum((local < 0).astype(jnp.int32), axis=-1)
    counts = jnp.sum(((local >= 0) & (local < blocks_here)).astype(jnp.int32), axis=-1)
    slots = jnp.arange(MOST, dtype=jnp.int32)
    places = jnp.arange(blocks.shape[-1], dtype=jnp.int32)
    here = places == ((below + counts - 1)[..., None] - slots)[..., None]
    picked = jnp.sum(jnp.where(here, local[:, :, None, :], 0), axis=-1)
    picked = jnp.clip(picked, 0, blocks_here - 1)
    query_block = jnp.arange(blocks.shape[0], dtype=jnp.int32)[:, None]
    diagonal = picked[..., 0] + shard_first == diag_first + query_block
    barred = jnp.where(slots == 0, diagonal[..., None], slots >= counts[..., None])
    return picked, jnp.where(barred, -jnp.inf, 0.0).astype(jnp.float32)


def on_device(queries, key_cache, value_cache, blocks, out_weight):
    head_count = key_cache.shape[1] // HD
    shards, groups = lax.axis_size("ctx"), lax.axis_size("kv")
    blocks_here = key_cache.shape[0] // BLK
    shard_first = lax.axis_index("ctx") * blocks_here
    diag_first = shards * blocks_here - queries.shape[0] * shards // BLK
    picked, biases = choose(blocks, head_count, shard_first, blocks_here, diag_first)
    keys = key_cache.reshape(blocks_here, BLK, -1)
    values = value_cache.reshape(blocks_here, BLK, -1)
    return layer(queries, keys, values, picked, biases, out_weight, shards, groups)


def solution(mesh):
    placed = (P("ctx", "kv"), P("ctx", "kv"), P("ctx", "kv"), P(), P("kv", "ctx"))
    return jax.shard_map(
        on_device, mesh=mesh, in_specs=placed, out_specs=P("kv", "ctx"), check_vma=False
    )
```

```python
import math

import jax
import jax.numpy as jnp
from jax import lax
from jax.experimental import pallas as pl
from jax.experimental.pallas import tpu as pltpu
from jax.sharding import PartitionSpec as P

HD = 128
BLK = 128
MOST = 7
LOG2E = math.log2(math.e)
MESH = pl.DeviceIdType.MESH


def layer_kernel(
    shards,
    groups,
    picked,
    biases,
    q_ref,
    k_ref,
    v_ref,
    w_hbm,
    out_ref,
    q_all,
    part,
    part_lse,
    pair_in,
    pair_lse,
    stage,
    stage_lse,
    chip_in,
    chip_lse,
    merged_all,
    weight,
    projected,
    group_in,
    corner_in,
    q_send,
    q_recv,
    m_send,
    m_recv,
    pair_send,
    pair_recv,
    pair_lse_send,
    pair_lse_recv,
    chip_send,
    chip_recv,
    chip_lse_send,
    chip_lse_recv,
    group_send,
    group_recv,
    corner_recv,
    w_sem,
):
    me, group_me = lax.axis_index("ctx"), lax.axis_index("kv")
    chips = shards // 2
    chip, core = me // 2, me % 2
    partner = chip * 2 + 1 - core
    tokens = q_ref.shape[0]
    columns = q_ref.shape[1]
    heads = columns // HD
    lists = k_ref.shape[2] // HD
    per_list = heads // lists
    per_group = shards // groups
    scale = LOG2E / math.sqrt(HD)

    weight_copy = pltpu.make_async_copy(w_hbm, weight, w_sem)
    weight_copy.start()

    barrier = pltpu.get_barrier_semaphore()
    pl.semaphore_signal(barrier, inc=1, device_id={"ctx": partner}, device_id_type=MESH)
    for step in range(1, chips):
        other = lax.rem(chip + step, chips) * 2 + core
        pl.semaphore_signal(barrier, inc=1, device_id={"ctx": other}, device_id_type=MESH)
    for step in range(1, groups):
        other = lax.rem(group_me + step, groups)
        pl.semaphore_signal(barrier, inc=1, device_id={"kv": other}, device_id_type=MESH)
    pl.semaphore_wait(barrier, chips + groups - 1)

    def remote(source, target, send, recv, where):
        return pltpu.make_async_remote_copy(
            src_ref=source,
            dst_ref=target,
            send_sem=send,
            recv_sem=recv,
            device_id=where,
            device_id_type=MESH,
        )

    def along(buffer, send, recv, slot, way):
        target = {0: me + 2, 1: me - 2, 2: partner}[way]
        return remote(
            buffer.at[slot], buffer.at[slot], send.at[way, slot], recv.at[slot], {"ctx": target}
        )

    def spread(buffer, send, recv, step):
        def pass_on(slot, way, allowed):
            @pl.when(allowed)
            def _():
                along(buffer, send, recv, slot, way).start()

        low, high = chip - step, chip + step

        @pl.when(low >= 0)
        def _():
            slot = low * 2 + core

            @pl.when(step > 0)
            def _():
                along(buffer, send, recv, slot, 0).wait_recv()

            pass_on(slot, 0, chip + 1 < chips)
            pass_on(slot, 2, step >= 0)

        @pl.when(high < chips)
        def _():
            slot = high * 2 + core

            @pl.when(step > 0)
            def _():
                along(buffer, send, recv, slot, 1).wait_recv()

            pass_on(slot, 1, chip >= 1)
            pass_on(slot, 2, step > 0)

    def finish_spread(buffer, send, recv):
        def one(at, carry):
            slot = at * 2 + core

            @pl.when((at <= chip) & (chip + 1 < chips))
            def _():
                along(buffer, send, recv, slot, 0).wait_send()

            @pl.when((at >= chip) & (chip >= 1))
            def _():
                along(buffer, send, recv, slot, 1).wait_send()

            along(buffer, send, recv, slot, 2).wait_send()
            return carry

        lax.fori_loop(0, chips, one, 0)

    def pair_copies(at):
        slot = at * 2 + 1 - core
        where = {"ctx": partner}
        return (
            remote(part.at[slot], pair_in.at[at], pair_send.at[at], pair_recv.at[at], where),
            remote(
                part_lse.at[slot],
                pair_lse.at[at],
                pair_lse_send.at[at],
                pair_lse_recv.at[at],
                where,
            ),
        )

    def chip_copies(source, target):
        where = {"ctx": target * 2 + core}
        return (
            remote(
                stage.at[target],
                chip_in.at[source],
                chip_send.at[target],
                chip_recv.at[source],
                where,
            ),
            remote(
                stage_lse.at[target],
                chip_lse.at[source],
                chip_lse_send.at[target],
                chip_lse_recv.at[source],
                where,
            ),
        )

    beside = group_me + 1 - 2 * (group_me % 2)
    across = (group_me + 2) % 4
    corner = 3 - group_me

    def group_copy(slot):
        owner, inside = slot // per_group, slot % per_group
        source = jnp.where(owner == beside, 0, 1)
        return remote(
            projected.at[slot],
            group_in.at[source, inside],
            group_send.at[slot],
            group_recv.at[source, inside],
            {"kv": owner},
        )

    def corner_copy(at, half):
        return remote(
            projected.at[at * 2 + half],
            corner_in.at[at],
            group_send.at[at * 2 + half],
            corner_recv.at[at],
            {"kv": across if half else beside},
        )

    def send_projected(at):
        owner = at * 2 // per_group

        @pl.when(owner == corner)
        def _():
            corner_copy(at, 0).start()
            corner_copy(at, 1).start()

        @pl.when(owner == beside)
        def _():
            group_copy(at * 2).start()

        @pl.when(owner == across)
        def _():
            group_copy(at * 2 + 1).start()

    def send_joined(at):
        owner = at * 2 // per_group

        @pl.when((owner == beside) | (owner == across))
        def _():
            corner_copy(at, 0).wait_recv()
            slot = at * 2 + jnp.where(owner == beside, 1, 0)
            joined = projected[slot].astype(jnp.float32) + corner_in[at].astype(jnp.float32)
            projected[slot] = joined.astype(jnp.bfloat16)
            group_copy(slot).start()

    def join_step(step):
        @pl.when((step >= 0) & (chip - step >= 0))
        def _():
            send_joined(chip - step)

        @pl.when((step > 0) & (chip + step < chips))
        def _():
            send_joined(chip + step)

    def attend(slot):
        first = slot * tokens
        block_index, offset = first // BLK, first % BLK
        stack = max(1, min(per_list, 2 * BLK // tokens))
        rows = lax.broadcasted_iota(jnp.int32, (stack * tokens, BLK), 0) % tokens + offset
        places = lax.broadcasted_iota(jnp.int32, (stack * tokens, BLK), 1)
        lanes = lax.broadcasted_iota(jnp.int32, (tokens, BLK), 1)
        stats = jnp.zeros((tokens, BLK), jnp.float32)
        for index in range(lists):
            chosen = [picked[block_index, index, at] for at in range(MOST)]
            bias = [biases[block_index, index, at] for at in range(MOST)]
            causal = jnp.where(places > rows, bias[0], 0.0)
            here = slice(index * HD, (index + 1) * HD)
            keys = jnp.concatenate([k_ref[one, :, here] for one in chosen], 0)
            values = jnp.concatenate([v_ref[one, :, here] for one in chosen], 0)
            for begin in range(index * per_list, (index + 1) * per_list, stack):
                at = [slice(g * HD, (g + 1) * HD) for g in range(begin, begin + stack)]
                queries = jnp.concatenate([q_all[slot, :, a] for a in at], 0)
                scores = lax.dot_general(
                    queries, keys, (((1,), (1,)), ((), ())), preferred_element_type=jnp.float32
                )
                pieces = [scores[:, :BLK] + causal]
                for s in range(1, MOST):
                    pieces.append(scores[:, s * BLK : (s + 1) * BLK] + bias[s])
                scores = jnp.concatenate(pieces, 1)
                peak = jnp.max(scores, axis=1, keepdims=True) * scale
                weights = jnp.exp2(scores * scale - peak)
                total = jnp.sum(weights, axis=1, keepdims=True)
                mixed = jnp.dot(
                    weights.astype(jnp.bfloat16), values, preferred_element_type=jnp.float32
                )
                mixed = (mixed / total).astype(jnp.bfloat16)
                lse = peak + jnp.log2(total)
                for i in range(stack):
                    mine = slice(i * tokens, (i + 1) * tokens)
                    part[slot, :, at[i]] = mixed[mine]
                    stats = jnp.where(lanes == begin + i, lse[mine], stats)
        part_lse[slot] = stats.T[:heads]

    def merge_pair(at):
        slot = at * 2 + core
        for copy in pair_copies(at):
            copy.wait_recv()
        own, other = part_lse[slot], pair_lse[at]
        top = jnp.maximum(own, other)
        own, other = jnp.exp2(own - top), jnp.exp2(other - top)
        total = own + other
        joint = top + jnp.log2(total)
        own, other = (own / total).T, (other / total).T

        def store(to, to_lse, place):
            to_lse[place] = joint
            for g in range(heads):
                a = slice(g * HD, (g + 1) * HD)
                both = own[:, g : g + 1] * part[slot, :, a].astype(jnp.float32)
                both += other[:, g : g + 1] * pair_in[at, :, a].astype(jnp.float32)
                to[place, :, a] = both.astype(jnp.bfloat16)

        @pl.when(at == chip)
        def _():
            store(chip_in, chip_lse, chip)

        @pl.when(at != chip)
        def _():
            store(stage, stage_lse, at)
            for copy in chip_copies(chip, at):
                copy.start()

    def two_sides(step, visit, between):
        def one(turn, carry):
            side = jnp.where(chip - step >= 0, turn, 1 - turn)
            at = jnp.where(side == 0, chip - step, chip + step)

            @pl.when((at >= 0) & (at < chips) & ((step > 0) | (turn == 0)))
            def _():
                visit(at)

            @pl.when(turn == 0)
            def _():
                between(step + 1)

            return carry

        lax.fori_loop(0, 2, one, 0)

    q_all[me] = q_ref[...]
    spread(q_all, q_send, q_recv, 0)

    def attend_chip(at):
        def one(own_core, carry):
            slot = at * 2 + jnp.where(own_core == 1, core, 1 - core)

            @pl.when(own_core == 0)
            def _():
                along(q_all, q_send, q_recv, slot, 2).wait_recv()

            attend(slot)

            @pl.when(own_core == 0)
            def _():
                for copy in pair_copies(at):
                    copy.start()

            return carry

        lax.fori_loop(0, 2, one, 0)
        merge_pair(at)

    def attend_step(step, carry):
        two_sides(step, attend_chip, lambda later: spread(q_all, q_send, q_recv, later))
        return carry

    lax.fori_loop(0, chips, attend_step, 0)

    def receive(step, carry):
        source = lax.rem(chip + step, chips)
        for copy in chip_copies(source, chip):
            copy.wait_recv()
        return carry

    lax.fori_loop(1, chips, receive, 0)
    top = chip_lse[0]
    for c in range(1, chips):
        top = jnp.maximum(top, chip_lse[c])
    shares = [jnp.exp2(chip_lse[c] - top) for c in range(chips)]
    total = shares[0]
    for c in range(1, chips):
        total = total + shares[c]
    shares = [(share / total).T for share in shares]
    for g in range(heads):
        a = slice(g * HD, (g + 1) * HD)
        summed = shares[0][:, g : g + 1] * chip_in[0, :, a].astype(jnp.float32)
        for c in range(1, chips):
            summed += shares[c][:, g : g + 1] * chip_in[c, :, a].astype(jnp.float32)
        merged_all[me, :, a] = summed.astype(jnp.bfloat16)

    weight_copy.wait()

    spread(merged_all, m_send, m_recv, 0)

    def project_chip(at):
        along(merged_all, m_send, m_recv, at * 2 + 1 - core, 2).wait_recv()
        both = pl.ds(at * 2, 2)
        product = jnp.dot(
            merged_all[both].reshape(2 * tokens, columns),
            weight[...],
            preferred_element_type=jnp.float32,
        )
        projected[both] = product.astype(jnp.bfloat16).reshape(2, tokens, -1)

        send_projected(at)

    def project_step(step, carry):
        two_sides(step, project_chip, lambda later: spread(merged_all, m_send, m_recv, later))
        join_step(step - 1)
        return carry

    lax.fori_loop(0, chips, project_step, 0)
    join_step(chips - 1)

    def gather_groups(inside, carry):
        total = projected[group_me * per_group + inside].astype(jnp.float32)
        for source in range(2):
            arrived = group_in.at[source, inside]
            remote(
                arrived, arrived, group_send.at[0], group_recv.at[source, inside], {"kv": beside}
            ).wait_recv()
            total += group_in[source, inside].astype(jnp.float32)
        out_ref[pl.ds(pl.multiple_of(inside * tokens, tokens), tokens), :] = total.astype(
            out_ref.dtype
        )
        return carry

    lax.fori_loop(0, per_group, gather_groups, 0)

    finish_spread(q_all, q_send, q_recv)
    finish_spread(merged_all, m_send, m_recv)

    def finish_chips(at, carry):
        for copy in pair_copies(at):
            copy.wait_send()

        @pl.when(at != chip)
        def _():
            for copy in chip_copies(chip, at):
                copy.wait_send()

        return carry

    lax.fori_loop(0, chips, finish_chips, 0)

    def finish_groups(slot, carry):
        @pl.when(slot // per_group != group_me)
        def _():
            group_copy(slot).wait_send()

        return carry

    lax.fori_loop(0, shards, finish_groups, 0)


def layer(queries, keys, values, picked, biases, out_weight, shards, groups):
    tokens, columns = queries.shape
    heads = columns // HD
    chips = shards // 2
    wide = out_weight.shape[1]
    per_group = shards // groups
    half, full = jnp.bfloat16, jnp.float32
    dma = pltpu.SemaphoreType.DMA
    smem = pl.BlockSpec(memory_space=pltpu.SMEM)
    vmem = pl.BlockSpec(memory_space=pltpu.VMEM)

    def body(*refs):
        layer_kernel(shards, groups, *refs)

    return pl.pallas_call(
        body,
        in_specs=[smem] * 2 + [vmem] * 3 + [pl.BlockSpec(memory_space=pl.ANY)],
        out_specs=vmem,
        out_shape=jax.ShapeDtypeStruct((per_group * tokens, wide), half),
        scratch_shapes=[
            pltpu.VMEM((shards, tokens, columns), half),
            pltpu.VMEM((shards, tokens, columns), half),
            pltpu.VMEM((shards, heads, tokens), full),
            pltpu.VMEM((chips, tokens, columns), half),
            pltpu.VMEM((chips, heads, tokens), full),
            pltpu.VMEM((chips, tokens, columns), half),
            pltpu.VMEM((chips, heads, tokens), full),
            pltpu.VMEM((chips, tokens, columns), half),
            pltpu.VMEM((chips, heads, tokens), full),
            pltpu.VMEM((shards, tokens, columns), half),
            pltpu.VMEM(out_weight.shape, half),
            pltpu.VMEM((shards, tokens, wide), half),
            pltpu.VMEM((2, per_group, tokens, wide), half),
            pltpu.VMEM((chips, tokens, wide), half),
            dma((3, shards)),
            dma((shards,)),
            dma((3, shards)),
            dma((shards,)),
            dma((chips,)),
            dma((chips,)),
            dma((chips,)),
            dma((chips,)),
            dma((chips,)),
            dma((chips,)),
            dma((chips,)),
            dma((chips,)),
            dma((shards,)),
            dma((2, per_group)),
            dma((chips,)),
            dma,
        ],
        compiler_params=pltpu.CompilerParams(
            collective_id=0, has_side_effects=True, vmem_limit_bytes=56 * 2**20
        ),
        name="layer",
    )(picked, biases, queries, keys, values, out_weight)


def choose(blocks, head_count, shard_first, blocks_here, diag_first):
    lists = lax.dynamic_slice_in_dim(blocks, lax.axis_index("kv") * head_count, head_count, 1)
    local = lists - shard_first
    below = jnp.sum((local < 0).astype(jnp.int32), axis=-1)
    counts = jnp.sum(((local >= 0) & (local < blocks_here)).astype(jnp.int32), axis=-1)
    slots = jnp.arange(MOST, dtype=jnp.int32)
    places = jnp.arange(blocks.shape[-1], dtype=jnp.int32)
    here = places == ((below + counts - 1)[..., None] - slots)[..., None]
    picked = jnp.sum(jnp.where(here, local[:, :, None, :], 0), axis=-1)
    picked = jnp.clip(picked, 0, blocks_here - 1)
    query_block = jnp.arange(blocks.shape[0], dtype=jnp.int32)[:, None]
    diagonal = picked[..., 0] + shard_first == diag_first + query_block
    barred = jnp.where(slots == 0, diagonal[..., None], slots >= counts[..., None])
    return picked, jnp.where(barred, -jnp.inf, 0.0).astype(jnp.float32)


def on_device(queries, key_cache, value_cache, blocks, out_weight):
    head_count = key_cache.shape[1] // HD
    shards, groups = lax.axis_size("ctx"), lax.axis_size("kv")
    blocks_here = key_cache.shape[0] // BLK
    shard_first = lax.axis_index("ctx") * blocks_here
    diag_first = shards * blocks_here - queries.shape[0] * shards // BLK
    picked, biases = choose(blocks, head_count, shard_first, blocks_here, diag_first)
    keys = key_cache.reshape(blocks_here, BLK, -1)
    values = value_cache.reshape(blocks_here, BLK, -1)
    return layer(queries, keys, values, picked, biases, out_weight, shards, groups)


def solution(mesh):
    placed = (P("ctx", "kv"), P("ctx", "kv"), P("ctx", "kv"), P(), P("kv", "ctx"))
    return jax.shard_map(
        on_device, mesh=mesh, in_specs=placed, out_specs=P("kv", "ctx"), check_vma=False
    )
```

```python
import math

import jax
import jax.numpy as jnp
from jax import lax
from jax.experimental import pallas as pl
from jax.experimental.pallas import tpu as pltpu
from jax.sharding import PartitionSpec as P

HD = 128
BLK = 128
MOST = 7
LOG2E = math.log2(math.e)
MESH = pl.DeviceIdType.MESH


def layer_kernel(
    shards,
    groups,
    picked,
    biases,
    q_ref,
    k_ref,
    v_ref,
    w_hbm,
    out_ref,
    q_all,
    part,
    part_lse,
    pair_in,
    pair_lse,
    stage,
    stage_lse,
    chip_in,
    chip_lse,
    merged_all,
    weight,
    projected,
    group_in,
    corner_in,
    q_send,
    q_recv,
    m_send,
    m_recv,
    pair_send,
    pair_recv,
    pair_lse_send,
    pair_lse_recv,
    chip_send,
    chip_recv,
    chip_lse_send,
    chip_lse_recv,
    group_send,
    group_recv,
    corner_recv,
    w_sem,
):
    me, group_me = lax.axis_index("ctx"), lax.axis_index("kv")
    chips = shards // 2
    chip, core = me // 2, me % 2
    partner = chip * 2 + 1 - core
    tokens = q_ref.shape[0]
    columns = q_ref.shape[1]
    heads = columns // HD
    lists = k_ref.shape[2] // HD
    per_list = heads // lists
    per_group = shards // groups
    scale = LOG2E / math.sqrt(HD)

    weight_copy = pltpu.make_async_copy(w_hbm, weight, w_sem)
    weight_copy.start()

    barrier = pltpu.get_barrier_semaphore()
    pl.semaphore_signal(barrier, inc=1, device_id={"ctx": partner}, device_id_type=MESH)
    for step in range(1, chips):
        other = lax.rem(chip + step, chips) * 2 + core
        pl.semaphore_signal(barrier, inc=1, device_id={"ctx": other}, device_id_type=MESH)
    for step in range(1, groups):
        other = lax.rem(group_me + step, groups)
        pl.semaphore_signal(barrier, inc=1, device_id={"kv": other}, device_id_type=MESH)
    pl.semaphore_wait(barrier, chips + groups - 1)

    def remote(source, target, send, recv, where):
        return pltpu.make_async_remote_copy(
            src_ref=source,
            dst_ref=target,
            send_sem=send,
            recv_sem=recv,
            device_id=where,
            device_id_type=MESH,
        )

    def along(buffer, send, recv, slot, way):
        target = {0: me + 2, 1: me - 2, 2: partner}[way]
        return remote(
            buffer.at[slot], buffer.at[slot], send.at[way, slot], recv.at[slot], {"ctx": target}
        )

    def spread(buffer, send, recv, step):
        def pass_on(slot, way, allowed):
            @pl.when(allowed)
            def _():
                along(buffer, send, recv, slot, way).start()

        low, high = chip - step, chip + step

        @pl.when(low >= 0)
        def _():
            slot = low * 2 + core

            @pl.when(step > 0)
            def _():
                along(buffer, send, recv, slot, 0).wait_recv()

            pass_on(slot, 0, chip + 1 < chips)
            pass_on(slot, 2, step >= 0)

        @pl.when(high < chips)
        def _():
            slot = high * 2 + core

            @pl.when(step > 0)
            def _():
                along(buffer, send, recv, slot, 1).wait_recv()

            pass_on(slot, 1, chip >= 1)
            pass_on(slot, 2, step > 0)

    def finish_spread(buffer, send, recv):
        def one(at, carry):
            slot = at * 2 + core

            @pl.when((at <= chip) & (chip + 1 < chips))
            def _():
                along(buffer, send, recv, slot, 0).wait_send()

            @pl.when((at >= chip) & (chip >= 1))
            def _():
                along(buffer, send, recv, slot, 1).wait_send()

            along(buffer, send, recv, slot, 2).wait_send()
            return carry

        lax.fori_loop(0, chips, one, 0)

    def pair_copies(at):
        slot = at * 2 + 1 - core
        where = {"ctx": partner}
        return (
            remote(part.at[slot], pair_in.at[at], pair_send.at[at], pair_recv.at[at], where),
            remote(
                part_lse.at[slot],
                pair_lse.at[at],
                pair_lse_send.at[at],
                pair_lse_recv.at[at],
                where,
            ),
        )

    def chip_copies(source, target):
        where = {"ctx": target * 2 + core}
        return (
            remote(
                stage.at[target],
                chip_in.at[source],
                chip_send.at[target],
                chip_recv.at[source],
                where,
            ),
            remote(
                stage_lse.at[target],
                chip_lse.at[source],
                chip_lse_send.at[target],
                chip_lse_recv.at[source],
                where,
            ),
        )

    beside = group_me + 1 - 2 * (group_me % 2)
    across = (group_me + 2) % 4
    corner = 3 - group_me

    def group_copy(slot):
        owner, inside = slot // per_group, slot % per_group
        source = jnp.where(owner == beside, 0, 1)
        return remote(
            projected.at[slot],
            group_in.at[source, inside],
            group_send.at[slot],
            group_recv.at[source, inside],
            {"kv": owner},
        )

    def corner_copy(at, half):
        return remote(
            projected.at[at * 2 + half],
            corner_in.at[at],
            group_send.at[at * 2 + half],
            corner_recv.at[at],
            {"kv": across if half else beside},
        )

    def send_projected(at):
        owner = at * 2 // per_group

        @pl.when(owner == corner)
        def _():
            corner_copy(at, 0).start()
            corner_copy(at, 1).start()

        @pl.when(owner == beside)
        def _():
            group_copy(at * 2).start()

        @pl.when(owner == across)
        def _():
            group_copy(at * 2 + 1).start()

    def send_joined(at):
        owner = at * 2 // per_group

        @pl.when((owner == beside) | (owner == across))
        def _():
            corner_copy(at, 0).wait_recv()
            slot = at * 2 + jnp.where(owner == beside, 1, 0)
            joined = projected[slot].astype(jnp.float32) + corner_in[at].astype(jnp.float32)
            projected[slot] = joined.astype(jnp.bfloat16)
            group_copy(slot).start()

    def join_step(step):
        @pl.when((step >= 0) & (chip - step >= 0))
        def _():
            send_joined(chip - step)

        @pl.when((step > 0) & (chip + step < chips))
        def _():
            send_joined(chip + step)

    def attend(slot):
        first = slot * tokens
        block_index, offset = first // BLK, first % BLK
        stack = max(1, min(per_list, 4 * BLK // tokens))
        rows = lax.broadcasted_iota(jnp.int32, (stack * tokens, BLK), 0) % tokens + offset
        places = lax.broadcasted_iota(jnp.int32, (stack * tokens, BLK), 1)
        lanes = lax.broadcasted_iota(jnp.int32, (tokens, BLK), 1)
        stats = jnp.zeros((tokens, BLK), jnp.float32)
        for index in range(lists):
            chosen = [picked[block_index, index, at] for at in range(MOST)]
            bias = [biases[block_index, index, at] for at in range(MOST)]
            causal = jnp.where(places > rows, bias[0], 0.0)
            here = slice(index * HD, (index + 1) * HD)
            keys = jnp.concatenate([k_ref[one, :, here] for one in chosen], 0)
            values = jnp.concatenate([v_ref[one, :, here] for one in chosen], 0)
            for begin in range(index * per_list, (index + 1) * per_list, stack):
                at = [slice(g * HD, (g + 1) * HD) for g in range(begin, begin + stack)]
                queries = jnp.concatenate([q_all[slot, :, a] for a in at], 0)
                scores = lax.dot_general(
                    queries, keys, (((1,), (1,)), ((), ())), preferred_element_type=jnp.float32
                )
                pieces = [scores[:, :BLK] + causal]
                for s in range(1, MOST):
                    pieces.append(scores[:, s * BLK : (s + 1) * BLK] + bias[s])
                scores = jnp.concatenate(pieces, 1)
                peak = jnp.max(scores, axis=1, keepdims=True) * scale
                weights = jnp.exp2(scores * scale - peak)
                total = jnp.sum(weights, axis=1, keepdims=True)
                mixed = jnp.dot(
                    weights.astype(jnp.bfloat16), values, preferred_element_type=jnp.float32
                )
                mixed = (mixed / total).astype(jnp.bfloat16)
                lse = peak + jnp.log2(total)
                for i in range(stack):
                    mine = slice(i * tokens, (i + 1) * tokens)
                    part[slot, :, at[i]] = mixed[mine]
                    stats = jnp.where(lanes == begin + i, lse[mine], stats)
        part_lse[slot] = stats.T[:heads]

    def merge_pair(at):
        slot = at * 2 + core
        for copy in pair_copies(at):
            copy.wait_recv()
        own, other = part_lse[slot], pair_lse[at]
        top = jnp.maximum(own, other)
        own, other = jnp.exp2(own - top), jnp.exp2(other - top)
        total = own + other
        joint = top + jnp.log2(total)
        own, other = (own / total).T, (other / total).T

        def store(to, to_lse, place):
            to_lse[place] = joint
            for g in range(heads):
                a = slice(g * HD, (g + 1) * HD)
                both = own[:, g : g + 1] * part[slot, :, a].astype(jnp.float32)
                both += other[:, g : g + 1] * pair_in[at, :, a].astype(jnp.float32)
                to[place, :, a] = both.astype(jnp.bfloat16)

        @pl.when(at == chip)
        def _():
            store(chip_in, chip_lse, chip)

        @pl.when(at != chip)
        def _():
            store(stage, stage_lse, at)
            for copy in chip_copies(chip, at):
                copy.start()

    def two_sides(step, visit, between):
        def one(turn, carry):
            side = jnp.where(chip - step >= 0, turn, 1 - turn)
            at = jnp.where(side == 0, chip - step, chip + step)

            @pl.when((at >= 0) & (at < chips) & ((step > 0) | (turn == 0)))
            def _():
                visit(at)

            @pl.when(turn == 0)
            def _():
                between(step + 1)

            return carry

        lax.fori_loop(0, 2, one, 0)

    q_all[me] = q_ref[...]
    spread(q_all, q_send, q_recv, 0)

    def attend_chip(at):
        def one(own_core, carry):
            slot = at * 2 + jnp.where(own_core == 1, core, 1 - core)

            @pl.when(own_core == 0)
            def _():
                along(q_all, q_send, q_recv, slot, 2).wait_recv()

            attend(slot)

            @pl.when(own_core == 0)
            def _():
                for copy in pair_copies(at):
                    copy.start()

            return carry

        lax.fori_loop(0, 2, one, 0)
        merge_pair(at)

    def attend_step(step, carry):
        two_sides(step, attend_chip, lambda later: spread(q_all, q_send, q_recv, later))
        return carry

    lax.fori_loop(0, chips, attend_step, 0)

    def receive(step, carry):
        source = lax.rem(chip + step, chips)
        for copy in chip_copies(source, chip):
            copy.wait_recv()
        return carry

    lax.fori_loop(1, chips, receive, 0)
    top = chip_lse[0]
    for c in range(1, chips):
        top = jnp.maximum(top, chip_lse[c])
    shares = [jnp.exp2(chip_lse[c] - top) for c in range(chips)]
    total = shares[0]
    for c in range(1, chips):
        total = total + shares[c]
    shares = [(share / total).T for share in shares]
    for g in range(heads):
        a = slice(g * HD, (g + 1) * HD)
        summed = shares[0][:, g : g + 1] * chip_in[0, :, a].astype(jnp.float32)
        for c in range(1, chips):
            summed += shares[c][:, g : g + 1] * chip_in[c, :, a].astype(jnp.float32)
        merged_all[me, :, a] = summed.astype(jnp.bfloat16)

    weight_copy.wait()

    spread(merged_all, m_send, m_recv, 0)

    def project_chip(at):
        along(merged_all, m_send, m_recv, at * 2 + 1 - core, 2).wait_recv()
        both = pl.ds(at * 2, 2)
        product = jnp.dot(
            merged_all[both].reshape(2 * tokens, columns),
            weight[...],
            preferred_element_type=jnp.float32,
        )
        projected[both] = product.astype(jnp.bfloat16).reshape(2, tokens, -1)

        send_projected(at)

    def project_step(step, carry):
        two_sides(step, project_chip, lambda later: spread(merged_all, m_send, m_recv, later))
        join_step(step - 1)
        return carry

    lax.fori_loop(0, chips, project_step, 0)
    join_step(chips - 1)

    def gather_groups(inside, carry):
        total = projected[group_me * per_group + inside].astype(jnp.float32)
        for source in range(2):
            arrived = group_in.at[source, inside]
            remote(
                arrived, arrived, group_send.at[0], group_recv.at[source, inside], {"kv": beside}
            ).wait_recv()
            total += group_in[source, inside].astype(jnp.float32)
        out_ref[pl.ds(pl.multiple_of(inside * tokens, tokens), tokens), :] = total.astype(
            out_ref.dtype
        )
        return carry

    lax.fori_loop(0, per_group, gather_groups, 0)

    finish_spread(q_all, q_send, q_recv)
    finish_spread(merged_all, m_send, m_recv)

    def finish_chips(at, carry):
        for copy in pair_copies(at):
            copy.wait_send()

        @pl.when(at != chip)
        def _():
            for copy in chip_copies(chip, at):
                copy.wait_send()

        return carry

    lax.fori_loop(0, chips, finish_chips, 0)

    def finish_groups(slot, carry):
        @pl.when(slot // per_group != group_me)
        def _():
            group_copy(slot).wait_send()

        return carry

    lax.fori_loop(0, shards, finish_groups, 0)


def layer(queries, keys, values, picked, biases, out_weight, shards, groups):
    tokens, columns = queries.shape
    heads = columns // HD
    chips = shards // 2
    wide = out_weight.shape[1]
    per_group = shards // groups
    half, full = jnp.bfloat16, jnp.float32
    dma = pltpu.SemaphoreType.DMA
    smem = pl.BlockSpec(memory_space=pltpu.SMEM)
    vmem = pl.BlockSpec(memory_space=pltpu.VMEM)

    def body(*refs):
        layer_kernel(shards, groups, *refs)

    return pl.pallas_call(
        body,
        in_specs=[smem] * 2 + [vmem] * 3 + [pl.BlockSpec(memory_space=pl.ANY)],
        out_specs=vmem,
        out_shape=jax.ShapeDtypeStruct((per_group * tokens, wide), half),
        scratch_shapes=[
            pltpu.VMEM((shards, tokens, columns), half),
            pltpu.VMEM((shards, tokens, columns), half),
            pltpu.VMEM((shards, heads, tokens), full),
            pltpu.VMEM((chips, tokens, columns), half),
            pltpu.VMEM((chips, heads, tokens), full),
            pltpu.VMEM((chips, tokens, columns), half),
            pltpu.VMEM((chips, heads, tokens), full),
            pltpu.VMEM((chips, tokens, columns), half),
            pltpu.VMEM((chips, heads, tokens), full),
            pltpu.VMEM((shards, tokens, columns), half),
            pltpu.VMEM(out_weight.shape, half),
            pltpu.VMEM((shards, tokens, wide), half),
            pltpu.VMEM((2, per_group, tokens, wide), half),
            pltpu.VMEM((chips, tokens, wide), half),
            dma((3, shards)),
            dma((shards,)),
            dma((3, shards)),
            dma((shards,)),
            dma((chips,)),
            dma((chips,)),
            dma((chips,)),
            dma((chips,)),
            dma((chips,)),
            dma((chips,)),
            dma((chips,)),
            dma((chips,)),
            dma((shards,)),
            dma((2, per_group)),
            dma((chips,)),
            dma,
        ],
        compiler_params=pltpu.CompilerParams(
            collective_id=0, has_side_effects=True, vmem_limit_bytes=56 * 2**20
        ),
        name="layer",
    )(picked, biases, queries, keys, values, out_weight)


def choose(blocks, head_count, shard_first, blocks_here, diag_first):
    lists = lax.dynamic_slice_in_dim(blocks, lax.axis_index("kv") * head_count, head_count, 1)
    local = lists - shard_first
    below = jnp.sum((local < 0).astype(jnp.int32), axis=-1)
    counts = jnp.sum(((local >= 0) & (local < blocks_here)).astype(jnp.int32), axis=-1)
    slots = jnp.arange(MOST, dtype=jnp.int32)
    places = jnp.arange(blocks.shape[-1], dtype=jnp.int32)
    here = places == ((below + counts - 1)[..., None] - slots)[..., None]
    picked = jnp.sum(jnp.where(here, local[:, :, None, :], 0), axis=-1)
    picked = jnp.clip(picked, 0, blocks_here - 1)
    query_block = jnp.arange(blocks.shape[0], dtype=jnp.int32)[:, None]
    diagonal = picked[..., 0] + shard_first == diag_first + query_block
    barred = jnp.where(slots == 0, diagonal[..., None], slots >= counts[..., None])
    return picked, jnp.where(barred, -jnp.inf, 0.0).astype(jnp.float32)


def on_device(queries, key_cache, value_cache, blocks, out_weight):
    head_count = key_cache.shape[1] // HD
    shards, groups = lax.axis_size("ctx"), lax.axis_size("kv")
    blocks_here = key_cache.shape[0] // BLK
    shard_first = lax.axis_index("ctx") * blocks_here
    diag_first = shards * blocks_here - queries.shape[0] * shards // BLK
    picked, biases = choose(blocks, head_count, shard_first, blocks_here, diag_first)
    keys = key_cache.reshape(blocks_here, BLK, -1)
    values = value_cache.reshape(blocks_here, BLK, -1)
    return layer(queries, keys, values, picked, biases, out_weight, shards, groups)


def solution(mesh):
    placed = (P("ctx", "kv"), P("ctx", "kv"), P("ctx", "kv"), P(), P("kv", "ctx"))
    return jax.shard_map(
        on_device, mesh=mesh, in_specs=placed, out_specs=P("kv", "ctx"), check_vma=False
    )
```
